32 devices in a mesh: prow: 4 (over x, core), pcol: 8 (over z, y).
Axes of the slice: x: 2, y: 2, z: 4, core: 2. Of those that a mesh axis runs over, the one named last changes fastest.
Arguments:
- tail_factor: float32 [63488, 2048], P(('prow', 'pcol')), may hold values from -0.0234375 to 0.0234375
- link_factor: float32 [1024, 1024], P(('prow', 'pcol')), may hold values from -0.1875 to 0.1875
- diag_inverse: float32 [2, 1024, 1024], P(None, ('prow', 'pcol')), as said below
- tail_solution: float32 [63488, 256], P(('prow', 'pcol')), may hold values from -6 to 6
- head_rhs: float32 [2, 1024, 256], P(None, ('prow', 'pcol')), may hold values from -6 to 6
- head_pivots: int32 [2, 1024], P(None, ('prow', 'pcol')), may hold values from 0 to 65535, as said below
- tail_pivots: int32 [63488], P(('prow', 'pcol')), may hold values from 0 to 65535, as said below
Outputs:
- solution: float32 [65536, 256], P(('prow', 'pcol'))
The draws below stay inside these ranges and needn't reach their ends.
Inputs may be any that keep to these rules, and one draw needn't show every extreme that they name: head_pivots and tail_pivots together are a permutation of the 65536 rows. Split the rows into 32 sets, set s holding rows s * 32 to (s + 1) * 32 - 1 of each head block and rows s * 1984 to (s + 1) * 1984 - 1 of tail_pivots, and the final rows into aligned blocks of 2048: each set sends at most 85 rows into each block, and every set sends exactly 85 into some block. `head_pivots`: part of the same permutation as tail_pivots. `diag_inverse`: unit upper triangular.
All inputs are finite; a program needn't handle non-finite values.
Results may differ from the reference program's by a relative error of at most 0.00007.
Values sent between devices are 32-bit elements; how exact they have to be, the bound alone decides.
A program may use at most 128 MiB of HBM per device.

```python
import jax
import jax.numpy as jnp
from jax import lax

B = 1024
RHS = 256
ROWS_DEV = 2048
DEVS = 32
HEAD_DEV = 32
NT = 63488


def pivot_table(key):
    even_count = ROWS_DEV // DEVS
    swing = max(even_count // 3, 1)
    first_key, second_key, third_key = jax.random.split(key, 3)
    shifted = jax.random.permutation(first_key, DEVS)
    columns = jnp.arange(DEVS, dtype=jnp.int32)
    plus_cell = (columns[None, :] == shifted[:, None]).astype(jnp.int32)
    minus_cell = (columns[None, :] == (shifted[:, None] + 1) % DEVS).astype(jnp.int32)
    counts = even_count + swing * (plus_cell - minus_cell)
    bounds = jnp.cumsum(counts, axis=1)
    positions = jnp.arange(ROWS_DEV, dtype=jnp.int32)
    target = jax.vmap(lambda edge: jnp.searchsorted(edge, positions, side='right').astype(jnp.int32))(bounds)
    row_keys = jax.random.split(second_key, DEVS)
    shuffled = jax.vmap(lambda one_key, values: jax.random.permutation(one_key, values))(row_keys, target)
    tiebreak = jax.random.permutation(third_key, DEVS * ROWS_DEV).astype(jnp.int32)
    score = shuffled.reshape(-1) * (DEVS * ROWS_DEV) + tiebreak
    order = jnp.argsort(score, stable=True)
    final_row = jnp.zeros((DEVS * ROWS_DEV,), jnp.int32).at[order].set(jnp.arange(DEVS * ROWS_DEV, dtype=jnp.int32))
    return final_row.reshape(DEVS, ROWS_DEV)


def draw_head_pivots(key, part):
    table = pivot_table(key)
    head_part = table[:, :2 * HEAD_DEV].reshape(DEVS, 2, HEAD_DEV)
    return jnp.transpose(head_part, (1, 0, 2)).reshape(2, B)


def draw_tail_pivots(key, part):
    table = pivot_table(key)
    return table[:, 2 * HEAD_DEV:].reshape(-1)


def draw_diag_inverse(key, part):
    key = jax.random.fold_in(key, 7)
    values = jax.random.normal(key, (2, B, B), jnp.float32) * (0.9 / B ** 0.5)
    return jnp.triu(values, 1) + jnp.eye(B, dtype=jnp.float32)[None, :, :]


def steps_of(stream_key, extent, cuts, least, top_value):
    factor_of = 1.0
    for dim, blocks in cuts:
        heights = jax.random.uniform(jax.random.fold_in(jax.random.fold_in(stream_key, 6), dim), (blocks,), jnp.float32, least / len(cuts), top_value / len(cuts))
        factor_of = factor_of * jnp.repeat(jnp.exp(heights), extent[dim] // blocks).reshape((-1,) + (1,) * (len(extent) - 1 - dim))
    return factor_of


def normal_values(key, shape, width, bound, pieces=(), kind=jnp.bfloat16):
    entries = jax.random.normal(key, shape, jnp.float32) * width
    if len(pieces) > 0:
        entries = steps_of(key, shape, pieces, -0.22, 0.18) * entries
    return jnp.clip(entries, min=-bound, max=bound).astype(kind)


def setup_inputs(seed: int = 0) -> dict:
    seeds = jax.random.split(jax.random.key(seed), 8)
    tail_factor = normal_values(seeds[0], (NT, 2 * B), NT ** -0.5, 0.0234375, ((0, 32),), jnp.float32)
    link_factor = normal_values(seeds[1], (B, B), B ** -0.5, 0.1875, ((0, 32),), jnp.float32)
    diag_inverse = draw_diag_inverse(jax.random.fold_in(seeds[7], 71), 0)
    tail_solution = normal_values(seeds[3], (NT, RHS), 1.0, 6.0, ((0, 32),), jnp.float32)
    head_rhs = normal_values(seeds[4], (2, B, RHS), 1.0, 6.0, ((1, 32),), jnp.float32)
    head_pivots = draw_head_pivots(jax.random.fold_in(seeds[7], 71), 0)
    tail_pivots = draw_tail_pivots(jax.random.fold_in(seeds[7], 71), 0)
    return {"tail_factor": tail_factor, "link_factor": link_factor, "diag_inverse": diag_inverse, "tail_solution": tail_solution, "head_rhs": head_rhs, "head_pivots": head_pivots, "tail_pivots": tail_pivots}


def reference(tail_factor, link_factor, diag_inverse, tail_solution, head_rhs, head_pivots, tail_pivots):
    highest = lax.Precision.HIGHEST
    tail_terms = jnp.einsum("jc,jr->cr", tail_factor, tail_solution, precision=highest)
    reduced_upper = head_rhs[1] - tail_terms[B:]
    upper = jnp.dot(diag_inverse[1], reduced_upper, precision=highest)
    reduced_lower = head_rhs[0] - tail_terms[:B] - jnp.einsum("ic,ir->cr", link_factor, upper, precision=highest)
    lower = jnp.dot(diag_inverse[0], reduced_lower, precision=highest)
    sweep = jnp.concatenate([lower, upper, tail_solution], axis=0)
    pivots = jnp.concatenate([head_pivots[0], head_pivots[1], tail_pivots]).astype(jnp.int32)
    return jnp.zeros_like(sweep).at[pivots].set(sweep)
```

```python
import functools

import jax
import jax.numpy as jnp
from jax import lax
from jax.experimental import pallas as pl
from jax.experimental.pallas import tpu as pltpu
from jax.sharding import PartitionSpec as P

AXES = ("prow", "pcol")
MESH = pl.DeviceIdType.MESH
HIGHEST = lax.Precision.HIGHEST


def levels_of(prow, pcol):
    cores = 2 if prow % 2 == 0 else 1
    depth = 4 if pcol % 4 == 0 else 1
    return prow // cores, cores, depth, pcol // depth


def dot32(a, b, contract):
    return lax.dot_general(
        a, b, (contract, ((), ())), precision=HIGHEST, preferred_element_type=jnp.float32
    )


def sweep_kernel(
    sizes, terms, link, diag, rhs, pivots, outgoing,
    received, heads, all_pivots,
    full_upper, full_lower, base, pick,
    up_recv, up_sum, low_recv, low_sum,
    send_sems, recv_sems, move_send, move_recv, own_sem,
):
    xs, cores, zs, ys = sizes
    prow, pcol = lax.axis_index("prow"), lax.axis_index("pcol")
    devices = xs * cores * zs * ys
    position = prow * (zs * ys) + pcol
    x, core = prow // cores, prow % cores
    z, y = pcol // ys, pcol % ys

    def at_core(v):
        return (x * cores + v, pcol)

    def at_x(v):
        return (v * cores + core, pcol)

    def at_y(v):
        return (prow, z * ys + v)

    def at_z(v):
        return (prow, v * ys + y)

    coords = {"c": (core, cores, at_core), "x": (x, xs, at_x), "y": (y, ys, at_y), "z": (z, zs, at_z)}
    counter = [0]

    def remote(src, dst, device):
        k = counter[0]
        counter[0] += 1
        copy = pltpu.make_async_remote_copy(
            src_ref=src, dst_ref=dst, send_sem=send_sems.at[k], recv_sem=recv_sems.at[k],
            device_id=device, device_id_type=MESH,
        )
        copy.start()
        return copy

    def reduce_start(axis, source, cut, landing):
        me, size, place = coords[axis]
        return [
            remote(cut(source, (me + d) % size), landing.at[d - 1], place((me + d) % size))
            for d in range(1, size)
        ]

    def gather_start(axis, ref):
        size = coords[axis][1]
        me, _, place = coords[axis]
        part = {
            "z": ref.at[x, core, z, y],
            "y": ref.at[x, core, :, y],
            "x": ref.at[x, core],
            "c": ref.at[:, core],
        }[axis]
        return [remote(part, part, place((me + d) % size)) for d in range(1, size)]

    def finish(copies):
        for copy in copies:
            copy.wait()

    cuts = {
        "c": lambda ref, v: ref.at[:, v],
        "x": lambda ref, v: ref.at[v],
        "y": lambda ref, v: ref.at[:, v],
        "z": lambda ref, v: ref.at[v],
    }
    reads = {
        "c": lambda ref: ref[:, core],
        "x": lambda ref: ref[x],
        "y": lambda ref: ref[:, y],
        "z": lambda ref: ref[z],
    }

    def reduce_levels(source, landings, sums, beside):
        current = source
        for step, axis in enumerate("cxyz"):
            size = coords[axis][1]
            copies = reduce_start(axis, current, cuts[axis], landings[step])
            others = [gather_start("zyxc"[step], ref) for ref in beside]
            finish(copies)
            total = reads[axis](current)
            for d in range(1, size):
                total = total + landings[step][d - 1]
            sums[step][...] = total
            for more in others:
                finish(more)
            current = sums[step]
        return current

    barrier = pltpu.get_barrier_semaphore()

    def greet(d, carry):
        peer = (position + d) % devices
        pl.semaphore_signal(
            barrier, inc=1, device_id=(peer // (zs * ys), peer % (zs * ys)), device_id_type=MESH
        )
        return carry

    lax.fori_loop(1, devices, greet, 0)
    pl.semaphore_wait(barrier, devices - 1)

    def move(d):
        peer = (position + d) % devices
        return pltpu.make_async_remote_copy(
            src_ref=outgoing.at[peer], dst_ref=received.at[position],
            send_sem=move_send.at[d], recv_sem=move_recv.at[d],
            device_id=(peer // (zs * ys), peer % (zs * ys)), device_id_type=MESH,
        )

    def move_start(d, carry):
        move(d).start()
        return carry

    def move_wait(d, carry):
        move(d).wait()
        return carry

    own = pltpu.make_async_copy(outgoing.at[position], received.at[position], own_sem)
    own.start()
    lax.fori_loop(1, devices, move_start, 0)

    all_pivots[x, core, z, y] = pivots[...]
    reduced = reduce_levels(terms.at[1], up_recv, up_sum, [all_pivots])
    full_upper[x, core, z, y] = rhs[1] - reduced[...]
    for axis in "zyxc":
        finish(gather_start(axis, full_upper))
    rows = devices * rhs.shape[1]
    columns = rhs.shape[2]
    upper = dot32(diag[1], full_upper[...].reshape(rows, columns), ((1,), (0,)))
    heads[1, x, core, z, y] = upper
    base[...] = terms[0] + dot32(link[...], upper, ((0,), (0,))).reshape(base.shape)
    reduced = reduce_levels(base, low_recv, low_sum, [heads.at[1]])
    full_lower[x, core, z, y] = rhs[0] - reduced[...]
    for axis in "zyxc":
        finish(gather_start(axis, full_lower))
    heads[0, x, core, z, y] = dot32(diag[0], full_lower[...].reshape(rows, columns), ((1,), (0,)))
    for axis in "zyxc":
        finish(gather_start(axis, heads.at[0]))

    own.wait()
    lax.fori_loop(1, devices, move_wait, 0)


def sweep_call(sizes, terms, link, diag, rhs, pivots, outgoing):
    xs, cores, zs, ys = sizes
    devices = xs * cores * zs * ys
    _, share, columns = rhs.shape
    tail = (share, columns)
    landings = lambda: [
        pltpu.VMEM((max(cores - 1, 1), xs, zs, ys) + tail, jnp.float32),
        pltpu.VMEM((max(xs - 1, 1), zs, ys) + tail, jnp.float32),
        pltpu.VMEM((max(ys - 1, 1), zs) + tail, jnp.float32),
        pltpu.VMEM((max(zs - 1, 1),) + tail, jnp.float32),
    ]
    sums = lambda: [
        pltpu.VMEM((xs, zs, ys) + tail, jnp.float32),
        pltpu.VMEM((zs, ys) + tail, jnp.float32),
        pltpu.VMEM((zs,) + tail, jnp.float32),
        pltpu.VMEM(tail, jnp.float32),
    ]
    whole = (xs, cores, zs, ys) + tail
    copies = 7 * ((cores - 1) + (xs - 1) + (zs - 1) + (ys - 1))
    vmem = pl.BlockSpec(memory_space=pltpu.VMEM)
    anywhere = pl.BlockSpec(memory_space=pl.ANY)
    return pl.pallas_call(
        functools.partial(sweep_kernel, sizes),
        out_shape=(
            jax.ShapeDtypeStruct(outgoing.shape, jnp.float32),
            jax.ShapeDtypeStruct((2,) + whole, jnp.float32),
            jax.ShapeDtypeStruct((xs, cores, zs, ys) + pivots.shape, jnp.int32),
        ),
        in_specs=[vmem] * 5 + [anywhere],
        out_specs=(anywhere, vmem, vmem),
        scratch_shapes=[
            pltpu.VMEM(whole, jnp.float32),
            pltpu.VMEM(whole, jnp.float32),
            pltpu.VMEM(whole, jnp.float32),
            pltpu.VMEM(tail, jnp.float32),
            landings(), sums(), landings(), sums(),
            pltpu.SemaphoreType.DMA((copies,)),
            pltpu.SemaphoreType.DMA((copies,)),
            pltpu.SemaphoreType.DMA((devices,)),
            pltpu.SemaphoreType.DMA((devices,)),
            pltpu.SemaphoreType.DMA,
        ],
        compiler_params=pltpu.CompilerParams(
            collective_id=0, has_side_effects=True, vmem_limit_bytes=40 * 2**20
        ),
    )(terms, link, diag, rhs, pivots, outgoing)


def pack_kernel(capacity, slots, rows, index_rows, out):
    def step(group, carry):
        start = pl.multiple_of(group * 8, 8)
        for k in range(8):
            out[pl.ds(slots[start + k], 1), :] = rows[pl.ds(start + k, 1), :]
        return carry

    lax.fori_loop(0, rows.shape[0] // 8, step, 0)
    devices = index_rows.shape[0]
    each = out.shape[0] // devices
    for d in range(devices):
        out[pl.ds(d * each + capacity, 1), :] = index_rows[pl.ds(d, 1), :]


def pack_call(capacity, each, slots, rows, index_rows):
    devices, columns = index_rows.shape
    return pl.pallas_call(
        functools.partial(pack_kernel, capacity),
        out_shape=jax.ShapeDtypeStruct((devices * each, columns), jnp.float32),
        in_specs=[
            pl.BlockSpec(memory_space=pltpu.SMEM),
            pl.BlockSpec(memory_space=pltpu.VMEM),
            pl.BlockSpec(memory_space=pltpu.VMEM),
        ],
        out_specs=pl.BlockSpec(memory_space=pltpu.VMEM),
        compiler_params=pltpu.CompilerParams(vmem_limit_bytes=24 * 2**20),
    )(slots, rows, index_rows)


def unpack_kernel(tail_slots, head_slots, received, heads, out, held, sem):
    def place(slots, source):
        def step(group, carry):
            start = pl.multiple_of(group * 8, 8)
            for k in range(8):
                held[pl.ds(slots[start + k], 1), :] = source[pl.ds(start + k, 1), :]
            return carry

        lax.fori_loop(0, source.shape[0] // 8, step, 0)

    place(tail_slots, received)
    place(head_slots, heads)
    copy = pltpu.make_async_copy(held.at[pl.ds(0, out.shape[0])], out, sem)
    copy.start()
    copy.wait()


def unpack_call(rows_each, tail_slots, head_slots, received, heads):
    columns = heads.shape[1]
    smem = pl.BlockSpec(memory_space=pltpu.SMEM)
    vmem = pl.BlockSpec(memory_space=pltpu.VMEM)
    return pl.pallas_call(
        unpack_kernel,
        out_shape=jax.ShapeDtypeStruct((rows_each, columns), jnp.float32),
        in_specs=[smem, smem, vmem, vmem],
        out_specs=pl.BlockSpec(memory_space=pl.ANY),
        scratch_shapes=[pltpu.VMEM((rows_each + 8, columns), jnp.float32), pltpu.SemaphoreType.DMA],
        compiler_params=pltpu.CompilerParams(vmem_limit_bytes=24 * 2**20),
    )(tail_slots, head_slots, received, heads)


def ranks_of(one_hot):
    rows, devices = one_hot.shape
    block = 128
    padded = -(-rows // block) * block
    blocks = jnp.pad(one_hot, ((0, padded - rows), (0, 0))).reshape(-1, block, devices)
    before = jnp.tril(jnp.ones((block, block), jnp.bfloat16), -1)
    inside = jnp.einsum("ij,bjd->bid", before, blocks, preferred_element_type=jnp.float32)
    totals = jnp.sum(blocks.astype(jnp.float32), axis=1)
    ahead = jnp.cumsum(totals, axis=0) - totals
    ranks = (inside + ahead[:, None, :]) * blocks.astype(jnp.float32)
    return jnp.sum(ranks, axis=2).reshape(-1)[:rows].astype(jnp.int32)


def body(tail_factor, link_factor, diag_inverse, tail_solution, head_rhs, head_pivots, tail_pivots):
    block_rows = diag_inverse.shape[2]
    share = diag_inverse.shape[1]
    tail_rows, columns = tail_solution.shape
    sizes = levels_of(lax.axis_size("prow"), lax.axis_size("pcol"))
    devices = lax.axis_size(AXES)
    position = lax.axis_index(AXES)
    rows_each = tail_rows + 2 * share
    even_count = rows_each // devices
    capacity = even_count + max(even_count // 3, 1)
    each = -(-(capacity + 1) // 8) * 8

    owner = tail_pivots // rows_each
    local_row = tail_pivots % rows_each
    one_hot = (owner[:, None] == jnp.arange(devices, dtype=jnp.int32)[None, :]).astype(jnp.bfloat16)
    rank = ranks_of(one_hot)
    slots = owner * each + rank
    at_rank = rank[:, None] == jnp.arange(columns, dtype=jnp.int32)[None, :]
    marked = local_row + 1
    high, low = marked // 64, marked % 64
    put = lambda v: jnp.dot(
        one_hot.T, jnp.where(at_rank, v[:, None], 0).astype(jnp.bfloat16),
        preferred_element_type=jnp.float32,
    )
    index_rows = put(high) * 64.0 + put(low)
    outgoing = pack_call(capacity, each, slots, tail_solution, index_rows)

    terms = jnp.einsum(
        "jc,jr->cr", tail_factor, tail_solution, precision=lax.Precision.HIGH
    )
    own_pivots = jnp.pad(head_pivots, ((0, 6), (0, 128 - share)))
    received, heads, all_pivots = sweep_call(
        sizes,
        terms.reshape((2,) + sizes + (share, columns)),
        link_factor, diag_inverse, head_rhs, own_pivots,
        outgoing.reshape(devices, each, columns),
    )
    marks = received[:, capacity, :each].astype(jnp.int32)
    inner = jnp.arange(each, dtype=jnp.int32)[None, :] < capacity
    tail_slots = jnp.where(inner & (marks > 0), marks - 1, rows_each).reshape(-1)
    pivots = all_pivots.reshape(devices, 8, 128)[:, :2, :share]
    head_slots = jnp.transpose(pivots, (1, 0, 2)).reshape(-1) - position * rows_each
    head_slots = jnp.where((head_slots >= 0) & (head_slots < rows_each), head_slots, rows_each)
    return unpack_call(
        rows_each, tail_slots, head_slots,
        received.reshape(-1, columns), heads.reshape(-1, columns),
    )


def solution(mesh):
    return jax.shard_map(
        body,
        mesh=mesh,
        in_specs=(
            P(AXES, None),
            P(AXES, None),
            P(None, AXES, None),
            P(AXES, None),
            P(None, AXES, None),
            P(None, AXES),
            P(AXES),
        ),
        out_specs=P(AXES, None),
        check_vma=False,
    )
```

```python
import functools
import itertools
import math

import jax
import jax.numpy as jnp
from jax import lax
from jax.experimental import pallas as pl
from jax.experimental.pallas import tpu as pltpu
from jax.sharding import PartitionSpec as P

AXES = ("prow", "pcol")
DIMS = "xczy"
LEVELS = ("c", "xy", "z")
BULK = 3
MESH = pl.DeviceIdType.MESH
HIGHEST = lax.Precision.HIGHEST


def levels_of(prow, pcol):
    cores = 2 if prow % 2 == 0 else 1
    depth = 4 if pcol % 4 == 0 else 1
    return prow // cores, cores, depth, pcol // depth


def dot32(a, b, contract):
    return lax.dot_general(
        a, b, (contract, ((), ())), precision=HIGHEST, preferred_element_type=jnp.float32
    )


def sweep_kernel(
    sizes, terms, link, diag, rhs, pivots, outgoing,
    received, heads, all_pivots,
    full_upper, full_lower, base, pick,
    up_recv, up_sum, low_recv, low_sum,
    send_sems, recv_sems, move_send, move_recv, own_sem,
):
    xs, cores, zs, ys = sizes
    prow, pcol = lax.axis_index("prow"), lax.axis_index("pcol")
    devices = xs * cores * zs * ys
    position = prow * (zs * ys) + pcol
    x, core = prow // cores, prow % cores
    z, y = pcol // ys, pcol % ys

    coord = {"x": x, "c": core, "z": z, "y": y}
    extent = {"x": xs, "c": cores, "z": zs, "y": ys}
    counter = [0]
    sent = [1]

    def more(count):
        first, last = sent[0], min(sent[0] + count, devices)
        sent[0] = last
        if last > first:
            lax.fori_loop(first, last, move_start, 0)

    def remote(src, dst, place):
        k = counter[0]
        counter[0] += 1
        copy = pltpu.make_async_remote_copy(
            src_ref=src, dst_ref=dst, send_sem=send_sems.at[k], recv_sem=recv_sems.at[k],
            device_id=(place["x"] * cores + place["c"], place["z"] * ys + place["y"]),
            device_id_type=MESH,
        )
        copy.start()
        return copy

    def peers(group):
        found = []
        for offsets in itertools.product(*[range(extent[a]) for a in group]):
            if any(offsets):
                place = dict(coord)
                for a, d in zip(group, offsets):
                    place[a] = (coord[a] + d) % extent[a]
                found.append(place)
        return found

    def cut(dims, group, place):
        return tuple(place[a] if a in group else slice(None) for a in dims)

    def gather_start(step, ref):
        group = LEVELS[::-1][step]
        waiting = "".join(LEVELS[: len(LEVELS) - step])
        part = ref.at[cut(DIMS, waiting, coord)]
        return [remote(part, part, place) for place in peers(group)]

    def finish(copies):
        for copy in copies:
            copy.wait()

    def gather(ref):
        for step in range(len(LEVELS)):
            copies = gather_start(step, ref)
            more(BULK)
            finish(copies)

    def reduce_levels(source, landings, sums, beside):
        current, dims = source, DIMS
        for step, group in enumerate(LEVELS):
            copies = [
                remote(current.at[cut(dims, group, place)], landings[step].at[n], place)
                for n, place in enumerate(peers(group))
            ]
            others = [gather_start(step, ref) for ref in beside]
            more(BULK)
            finish(copies)
            total = current[cut(dims, group, coord)]
            for n in range(len(copies)):
                total = total + landings[step][n]
            sums[step][...] = total
            for some in others:
                finish(some)
            current, dims = sums[step], "".join(a for a in dims if a not in group)
        return current

    barrier = pltpu.get_barrier_semaphore()

    def greet(d, carry):
        peer = (position + d) % devices
        pl.semaphore_signal(
            barrier, inc=1, device_id=(peer // (zs * ys), peer % (zs * ys)), device_id_type=MESH
        )
        return carry

    lax.fori_loop(1, devices, greet, 0)
    pl.semaphore_wait(barrier, devices - 1)

    def move(d):
        peer = (position + d) % devices
        return pltpu.make_async_remote_copy(
            src_ref=outgoing.at[peer], dst_ref=received.at[position],
            send_sem=move_send.at[d], recv_sem=move_recv.at[d],
            device_id=(peer // (zs * ys), peer % (zs * ys)), device_id_type=MESH,
        )

    def move_start(d, carry):
        move(d).start()
        return carry

    def move_wait(d, carry):
        move(d).wait()
        return carry

    own = pltpu.make_async_copy(outgoing.at[position], received.at[position], own_sem)
    own.start()

    all_pivots[x, core, z, y] = pivots[...]
    reduced = reduce_levels(terms.at[1], up_recv, up_sum, [all_pivots])
    full_upper[x, core, z, y] = rhs[1] - reduced[...]
    gather(full_upper)
    rows = devices * rhs.shape[1]
    columns = rhs.shape[2]
    upper = dot32(diag[1], full_upper[...].reshape(rows, columns), ((1,), (0,)))
    heads[1, x, core, z, y] = upper
    base[...] = terms[0] + dot32(link[...], upper, ((0,), (0,))).reshape(base.shape)
    reduced = reduce_levels(base, low_recv, low_sum, [heads.at[1]])
    full_lower[x, core, z, y] = rhs[0] - reduced[...]
    gather(full_lower)
    heads[0, x, core, z, y] = dot32(diag[0], full_lower[...].reshape(rows, columns), ((1,), (0,)))
    gather(heads.at[0])

    more(devices)
    own.wait()
    lax.fori_loop(1, devices, move_wait, 0)


def sweep_call(sizes, terms, link, diag, rhs, pivots, outgoing):
    xs, cores, zs, ys = sizes
    devices = xs * cores * zs * ys
    _, share, columns = rhs.shape
    tail = (share, columns)
    extent = {"x": xs, "c": cores, "z": zs, "y": ys}

    def buffers():
        landings, sums, dims, peers = [], [], DIMS, 0
        for group in LEVELS:
            dims = "".join(a for a in dims if a not in group)
            others = math.prod(extent[a] for a in group) - 1
            shape = tuple(extent[a] for a in dims) + tail
            landings.append(pltpu.VMEM((max(others, 1),) + shape, jnp.float32))
            sums.append(pltpu.VMEM(shape, jnp.float32))
            peers += others
        return landings, sums, peers

    up_recv, up_sum, peers = buffers()
    low_recv, low_sum, _ = buffers()
    whole = (xs, cores, zs, ys) + tail
    copies = 7 * peers
    vmem = pl.BlockSpec(memory_space=pltpu.VMEM)
    anywhere = pl.BlockSpec(memory_space=pl.ANY)
    return pl.pallas_call(
        functools.partial(sweep_kernel, sizes),
        out_shape=(
            jax.ShapeDtypeStruct(outgoing.shape, jnp.float32),
            jax.ShapeDtypeStruct((2,) + whole, jnp.float32),
            jax.ShapeDtypeStruct((xs, cores, zs, ys) + pivots.shape, jnp.int32),
        ),
        in_specs=[vmem] * 5 + [anywhere],
        out_specs=(anywhere, vmem, vmem),
        scratch_shapes=[
            pltpu.VMEM(whole, jnp.float32),
            pltpu.VMEM(whole, jnp.float32),
            pltpu.VMEM(whole, jnp.float32),
            pltpu.VMEM(tail, jnp.float32),
            up_recv, up_sum, low_recv, low_sum,
            pltpu.SemaphoreType.DMA((copies,)),
            pltpu.SemaphoreType.DMA((copies,)),
            pltpu.SemaphoreType.DMA((devices,)),
            pltpu.SemaphoreType.DMA((devices,)),
            pltpu.SemaphoreType.DMA,
        ],
        compiler_params=pltpu.CompilerParams(
            collective_id=0, has_side_effects=True, vmem_limit_bytes=40 * 2**20
        ),
    )(terms, link, diag, rhs, pivots, outgoing)


def pack_kernel(capacity, slots, rows, index_rows, out):
    def step(group, carry):
        start = pl.multiple_of(group * 8, 8)
        for k in range(8):
            out[pl.ds(slots[start + k], 1), :] = rows[pl.ds(start + k, 1), :]
        return carry

    lax.fori_loop(0, rows.shape[0] // 8, step, 0)
    devices = index_rows.shape[0]
    each = out.shape[0] // devices
    for d in range(devices):
        out[pl.ds(d * each + capacity, 1), :] = index_rows[pl.ds(d, 1), :]


def pack_call(capacity, each, slots, rows, index_rows):
    devices, columns = index_rows.shape
    return pl.pallas_call(
        functools.partial(pack_kernel, capacity),
        out_shape=jax.ShapeDtypeStruct((devices * each, columns), jnp.float32),
        in_specs=[
            pl.BlockSpec(memory_space=pltpu.SMEM),
            pl.BlockSpec(memory_space=pltpu.VMEM),
            pl.BlockSpec(memory_space=pltpu.VMEM),
        ],
        out_specs=pl.BlockSpec(memory_space=pltpu.VMEM),
        compiler_params=pltpu.CompilerParams(vmem_limit_bytes=24 * 2**20),
    )(slots, rows, index_rows)


def unpack_kernel(tail_slots, head_slots, tail_used, head_used, received, heads, out, held, sem):
    def place(slots, used, source):
        def step(group, carry):
            @pl.when(used[group] > 0)
            def _():
                start = pl.multiple_of(group * 8, 8)
                for k in range(8):
                    held[pl.ds(slots[start + k], 1), :] = source[pl.ds(start + k, 1), :]

            return carry

        lax.fori_loop(0, source.shape[0] // 8, step, 0)

    place(tail_slots, tail_used, received)
    place(head_slots, head_used, heads)
    copy = pltpu.make_async_copy(held.at[pl.ds(0, out.shape[0])], out, sem)
    copy.start()
    copy.wait()


def unpack_call(rows_each, tail_slots, head_slots, received, heads):
    columns = heads.shape[1]
    smem = pl.BlockSpec(memory_space=pltpu.SMEM)
    vmem = pl.BlockSpec(memory_space=pltpu.VMEM)

    def used(slots):
        return jnp.any(slots.reshape(-1, 8) < rows_each, axis=1).astype(jnp.int32)

    return pl.pallas_call(
        unpack_kernel,
        out_shape=jax.ShapeDtypeStruct((rows_each, columns), jnp.float32),
        in_specs=[smem] * 4 + [vmem, vmem],
        out_specs=pl.BlockSpec(memory_space=pl.ANY),
        scratch_shapes=[pltpu.VMEM((rows_each + 8, columns), jnp.float32), pltpu.SemaphoreType.DMA],
        compiler_params=pltpu.CompilerParams(vmem_limit_bytes=24 * 2**20),
    )(tail_slots, head_slots, used(tail_slots), used(head_slots), received, heads)


def ranks_of(one_hot):
    rows, devices = one_hot.shape
    block = 128
    padded = -(-rows // block) * block
    blocks = jnp.pad(one_hot, ((0, padded - rows), (0, 0))).reshape(-1, block, devices)
    before = jnp.tril(jnp.ones((block, block), jnp.bfloat16), -1)
    inside = jnp.einsum("ij,bjd->bid", before, blocks, preferred_element_type=jnp.float32)
    totals = jnp.sum(blocks.astype(jnp.float32), axis=1)
    ahead = jnp.cumsum(totals, axis=0) - totals
    ranks = (inside + ahead[:, None, :]) * blocks.astype(jnp.float32)
    return jnp.sum(ranks, axis=2).reshape(-1)[:rows].astype(jnp.int32)


def body(tail_factor, link_factor, diag_inverse, tail_solution, head_rhs, head_pivots, tail_pivots):
    block_rows = diag_inverse.shape[2]
    share = diag_inverse.shape[1]
    tail_rows, columns = tail_solution.shape
    sizes = levels_of(lax.axis_size("prow"), lax.axis_size("pcol"))
    devices = lax.axis_size(AXES)
    position = lax.axis_index(AXES)
    rows_each = tail_rows + 2 * share
    even_count = rows_each // devices
    capacity = even_count + max(even_count // 3, 1)
    each = -(-(capacity + 1) // 8) * 8

    owner = tail_pivots // rows_each
    local_row = tail_pivots % rows_each
    one_hot = (owner[:, None] == jnp.arange(devices, dtype=jnp.int32)[None, :]).astype(jnp.bfloat16)
    rank = ranks_of(one_hot)
    slots = owner * each + rank
    at_rank = rank[:, None] == jnp.arange(columns, dtype=jnp.int32)[None, :]
    marked = local_row + 1
    high, low = marked // 64, marked % 64
    put = lambda v: jnp.dot(
        one_hot.T, jnp.where(at_rank, v[:, None], 0).astype(jnp.bfloat16),
        preferred_element_type=jnp.float32,
    )
    index_rows = put(high) * 64.0 + put(low)
    outgoing = pack_call(capacity, each, slots, tail_solution, index_rows)

    terms = jnp.einsum(
        "jc,jr->cr", tail_factor, tail_solution, precision=lax.Precision.HIGH
    )
    own_pivots = jnp.pad(head_pivots, ((0, 6), (0, 128 - share)))
    received, heads, all_pivots = sweep_call(
        sizes,
        terms.reshape((2,) + sizes + (share, columns)),
        link_factor, diag_inverse, head_rhs, own_pivots,
        outgoing.reshape(devices, each, columns),
    )
    marks = received[:, capacity, :each].astype(jnp.int32)
    inner = jnp.arange(each, dtype=jnp.int32)[None, :] < capacity
    tail_slots = jnp.where(inner & (marks > 0), marks - 1, rows_each).reshape(-1)
    pivots = all_pivots.reshape(devices, 8, 128)[:, :2, :share]
    head_slots = jnp.transpose(pivots, (1, 0, 2)).reshape(-1) - position * rows_each
    head_slots = jnp.where((head_slots >= 0) & (head_slots < rows_each), head_slots, rows_each)
    return unpack_call(
        rows_each, tail_slots, head_slots,
        received.reshape(-1, columns), heads.reshape(-1, columns),
    )


def solution(mesh):
    return jax.shard_map(
        body,
        mesh=mesh,
        in_specs=(
            P(AXES, None),
            P(AXES, None),
            P(None, AXES, None),
            P(AXES, None),
            P(None, AXES, None),
            P(None, AXES),
            P(AXES),
        ),
        out_specs=P(AXES, None),
        check_vma=False,
    )
```
